32 devices in a mesh: groups: 2 (over y), dp: 4 (over z), tensor: 4 (over x, core).
Axes of the slice: x: 2, y: 2, z: 4, core: 2. Of those that a mesh axis runs over, the one named last changes fastest.
Arguments:
- tiles: bfloat16 [32, 256, 588], P(('groups', 'dp'), 'tensor'), parts along dimension 0, may hold values from -6 to 6
- tile_index: int32 [32], P(('groups', 'dp')), parts along dimension 0, may hold values from 0 to 3
- tile_from: int32 [16], P('groups'), parts along dimension 0, may hold values from 0 to 15, as said below
- patch_weight: bfloat16 [588, 1280], P(None, 'tensor'), may hold values from -0.25 to 0.25
- tile_table: float32 [4, 1280], replicated, may hold values from -3 to 3
- ln1_gain: float32 [1280], replicated, may hold values from 0.25 to 1.75
- ln1_bias: float32 [1280], replicated, may hold values from -1.5 to 1.5
- qkv_weight: bfloat16 [1280, 3, 1280], P(None, None, 'tensor'), may hold values from -32 to 32
- out_weight: bfloat16 [1280, 1280], P('tensor'), may hold values from -0.15625 to 0.15625
- ln2_gain: float32 [1280], replicated, may hold values from 0.25 to 1.75
- ln2_bias: float32 [1280], replicated, may hold values from -1.5 to 1.5
- fc1_weight: bfloat16 [1280, 5120], P(None, 'tensor'), may hold values from -0.15625 to 0.15625
- fc1_bias: float32 [5120], P('tensor'), may hold values from -1.5 to 1.5
- fc2_weight: bfloat16 [5120, 1280], P('tensor'), may hold values from -0.078125 to 0.078125
- fc2_bias: float32 [1280], replicated, may hold values from -1.5 to 1.5
- ln3_gain: float32 [1280], replicated, may hold values from 0.25 to 1.75
- ln3_bias: float32 [1280], replicated, may hold values from -1.5 to 1.5
- kv_weight: bfloat16 [1280, 2, 1024], P(None, None, 'tensor'), may hold values from -0.15625 to 0.15625
- knorm_gain: float32 [128], replicated, may hold values from 0.25 to 1.75
- page_owner: int32 [256], P(('groups', 'dp')), parts along dimension 0, may hold values from 0 to 3, as said below
- page_slot: int32 [256], P(('groups', 'dp')), parts along dimension 0, may hold values from 0 to 63, as said below
Outputs:
- cache: bfloat16 [512, 16, 2, 1024], P(('groups', 'dp'), None, None, 'tensor'), parts along dimension 0
The draws below stay inside these ranges and needn't reach their ends.
There are 2 independent parts, one for each index of `groups`. The reference program is written for one: setup_inputs(seed, part) draws one part's arguments, and reference() takes and returns one part's arrays. A program takes and returns all parts, laid end to end along the dimension named above; an argument that names none is the same for every part. Nothing has to cross between parts.
Inputs may be any that keep to these rules, and one draw needn't show every extreme that they name: `tile_from`: entry r * 2 + s names, as src * 4 + slot, the held tile that rank r encodes in its slot s. Every named tile is named once. A rank that encodes its own tile keeps it in place (s = slot < 2); a tile that changes rank comes from a slot 2 or higher. No rank hands more than 1 tiles to one other rank, and some pair reaches it; some rank holds 4 named tiles. Slots that are not named hold no work. `page_owner`: of the 32 pages of one rank at most 16 go to one owner, and some owner receives exactly 16 from every rank; no owner receives more than 64 pages. `page_slot`: pages with the same owner have different slots.
All inputs are finite; a program needn't handle non-finite values.
Results may differ from the reference program's by a relative error of at most 0.014.
Values may be sent and summed in bfloat16 or wider, within the bound.
A program may use at most 128 MiB of HBM per device.

```python
import jax
import jax.numpy as jnp
from jax import lax

D = 1280
HEADS = 16
HEAD_DIM = 80
FF = 5120
PATCH = 588
MAX_TILES = 4
KV_HEADS = 8
KV_DIM = 128
TILE_TOK = 256
BAL = 2
PAGE = 16
HOLD = 4
P_DEV = 32
PAGE_CAP = 16
CSLOTS = 64
TILES_IN = 16
N_DP = 4


def draw_tile_from(key, part):
    key = jax.random.fold_in(key, 11)
    rank_key = jax.random.fold_in(key, 101)
    count_key = jax.random.fold_in(key, 102)
    half = N_DP // 2
    scores = jax.random.randint(rank_key, (N_DP,), 0, 1 << 20).astype(jnp.int32) * N_DP + jnp.arange(N_DP, dtype=jnp.int32)
    ranking = jnp.argsort(scores, stable=True).astype(jnp.int32)
    surplus = jax.random.randint(count_key, (half,), 0, BAL + 1).astype(jnp.int32)
    surplus = surplus.at[0].set(BAL)
    places = jnp.arange(BAL, dtype=jnp.int32)
    members = jnp.arange(half, dtype=jnp.int32)
    heavy_rows = ranking[:half][:, None] * HOLD + places[None, :]
    source = (members[:, None] - places[None, :]) % half
    arriving = places[None, :] < surplus[source]
    owned = BAL - jnp.sum(arriving.astype(jnp.int32), axis=1)
    position = owned[:, None] + jnp.cumsum(arriving.astype(jnp.int32), axis=1) - 1
    offered = ranking[source] * HOLD + BAL + places[None, :]
    landing = arriving[:, :, None] & (position[:, :, None] == places[None, None, :])
    incoming = jnp.sum(jnp.where(landing, offered[:, :, None], 0), axis=1)
    kept = ranking[half:][:, None] * HOLD + places[None, :]
    light_rows = jnp.where(places[None, :] < owned[:, None], kept, incoming)
    table = jnp.zeros((N_DP, BAL), jnp.int32)
    table = table.at[ranking[:half]].set(heavy_rows).at[ranking[half:]].set(light_rows)
    return table.reshape(-1).astype(jnp.int32)


def page_plan(key):
    key = jax.random.fold_in(key, 23)
    owner_key, order_key, room_key, slot_key = jax.random.split(key, 4)
    hottest = jax.random.randint(owner_key, (), 0, N_DP).astype(jnp.int32)
    orders = jax.vmap(lambda single: jax.random.permutation(single, P_DEV))(jax.random.split(order_key, N_DP)).astype(jnp.int32)
    room_count = (N_DP - 1) * PAGE_CAP
    rooms = jax.vmap(lambda single: jax.random.permutation(single, room_count))(jax.random.split(room_key, N_DP)).astype(jnp.int32)
    extra = jnp.clip(orders - PAGE_CAP, 0, room_count - 1)
    picked = jnp.take_along_axis(rooms, extra, axis=1)
    spread = picked // PAGE_CAP
    others = spread + (spread >= hottest).astype(jnp.int32)
    owners = jnp.where(orders < PAGE_CAP, hottest, others).reshape(-1).astype(jnp.int32)
    hits = (owners[:, None] == jnp.arange(N_DP, dtype=jnp.int32)[None, :]).astype(jnp.int32)
    before = jnp.sum((jnp.cumsum(hits, axis=0) - hits) * hits, axis=1)
    shuffles = jax.vmap(lambda single: jax.random.permutation(single, CSLOTS))(jax.random.split(slot_key, N_DP)).astype(jnp.int32)
    slots = shuffles[owners, before]
    return (owners.astype(jnp.int32), slots.astype(jnp.int32))


def draw_page_owner(key, part):
    return page_plan(key)[0]


def draw_page_slot(key, part):
    return page_plan(key)[1]


def draw_qkv_weight(key, part):
    key = jax.random.fold_in(key, 5)
    base_key = jax.random.fold_in(key, 0)
    values = jnp.clip(jax.random.normal(base_key, (D, 3, HEADS * HEAD_DIM), jnp.float32), -6.0, 6.0) * D ** (-0.5)
    return values.astype(jnp.bfloat16)


def place_ends(values, key, least, largest):
    extent = values.shape
    index_at = [jax.random.randint(jax.random.fold_in(key, axis), (), 0, extent[axis]) for axis in range(len(extent))]
    values = values.at[tuple(index_at)].set(least)
    longest = extent.index(max(extent))
    index_at[longest] = (index_at[longest] + 1) % extent[longest]
    return values.at[tuple(index_at)].set(largest)


def block_levels(key, extent, cuts, smallest, top_value):
    def one(axis_at, shards_of):
        steps = jax.random.uniform(jax.random.fold_in(jax.random.fold_in(key, 6), axis_at), (shards_of,), jnp.float32, smallest / len(cuts), top_value / len(cuts))
        return jnp.repeat(jnp.exp(steps), extent[axis_at] // shards_of).reshape((-1,) + (1,) * (len(extent) - axis_at - 1))

    level = one(*cuts[0])
    for cut in cuts[1:]:
        level = level * one(*cut)
    return level


def bell_draw(key, dims, scale, most, pieces=(), kind=jnp.bfloat16):
    loudness = block_levels(key, dims, pieces, -0.22, 0.18) if pieces else 1.0
    result = jax.random.normal(key, dims, jnp.float32) * scale * loudness
    return jnp.minimum(jnp.maximum(result, -most), most).astype(kind)


def setup_inputs(seed: int = 0, part: int = 0) -> dict:
    streams_of = jax.random.split(jax.random.key(seed), 22)
    part_keys = jax.random.split(jax.random.fold_in(streams_of[21], part), 22)
    return {
        "tiles": bell_draw(part_keys[0], (TILES_IN, TILE_TOK, PATCH), 1.0, 6.0, ((0, 4), (1, 4))),
        "tile_index": place_ends(jax.random.randint(part_keys[1], (TILES_IN,), 0, MAX_TILES), jax.random.fold_in(part_keys[1], 1), 0, MAX_TILES - 1).astype(jnp.int32),
        "tile_from": draw_tile_from(jax.random.fold_in(jax.random.fold_in(streams_of[21], part), 71), part),
        "patch_weight": bell_draw(streams_of[3], (PATCH, D), PATCH ** -0.5, 0.25, ((1, 4),)),
        "tile_table": bell_draw(streams_of[4], (MAX_TILES, D), 0.5, 3.0, (), jnp.float32),
        "ln1_gain": jnp.clip(1.0 + 0.15 * jax.random.normal(streams_of[5], (D,), jnp.float32), 0.25, 1.75),
        "ln1_bias": bell_draw(streams_of[6], (D,), 0.3, 1.5, (), jnp.float32),
        "qkv_weight": draw_qkv_weight(jax.random.fold_in(streams_of[21], 71), part),
        "out_weight": bell_draw(streams_of[8], (HEADS * HEAD_DIM, D), (HEADS * HEAD_DIM) ** -0.5, 0.15625, ((0, 4),)),
        "ln2_gain": jnp.clip(1.0 + 0.15 * jax.random.normal(streams_of[9], (D,), jnp.float32), 0.25, 1.75),
        "ln2_bias": bell_draw(streams_of[10], (D,), 0.3, 1.5, (), jnp.float32),
        "fc1_weight": bell_draw(streams_of[11], (D, FF), D ** -0.5, 0.15625, ((1, 4),)),
        "fc1_bias": bell_draw(streams_of[12], (FF,), 0.3, 1.5, ((0, 4),), jnp.float32),
        "fc2_weight": bell_draw(streams_of[13], (FF, D), FF ** -0.5, 0.078125, ((0, 4),)),
        "fc2_bias": bell_draw(streams_of[14], (D,), 0.3, 1.5, (), jnp.float32),
        "ln3_gain": jnp.clip(1.0 + 0.15 * jax.random.normal(streams_of[15], (D,), jnp.float32), 0.25, 1.75),
        "ln3_bias": bell_draw(streams_of[16], (D,), 0.3, 1.5, (), jnp.float32),
        "kv_weight": bell_draw(streams_of[17], (D, 2, KV_HEADS * KV_DIM), D ** -0.5, 0.15625, ((2, 4),)),
        "knorm_gain": jnp.clip(1.0 + 0.15 * jax.random.normal(streams_of[18], (KV_DIM,), jnp.float32), 0.25, 1.75),
        "page_owner": draw_page_owner(jax.random.fold_in(jax.random.fold_in(streams_of[21], part), 71), part),
        "page_slot": draw_page_slot(jax.random.fold_in(jax.random.fold_in(streams_of[21], part), 71), part),
    }


def layer_norm(values, gain, bias):
    mean = lax.optimization_barrier(jnp.mean(values, axis=-1, keepdims=True))
    centred = values - mean
    spread = lax.optimization_barrier(jnp.mean(centred * centred, axis=-1, keepdims=True))
    return (centred * lax.rsqrt(spread + 1e-05) * gain + bias).astype(jnp.bfloat16)

def widen(values):
    return lax.optimization_barrier(values).astype(jnp.float32)

def encode_rank(pixels, positions, patch_weight, tile_table, ln1_gain, ln1_bias, qkv_weight, out_weight, ln2_gain, ln2_bias, fc1_weight, fc1_bias, fc2_weight, fc2_bias, ln3_gain, ln3_bias, kv_weight, knorm_gain):
    single = jnp.float32
    embedded = jnp.einsum('btp,pc->btc', pixels.astype(single), patch_weight.astype(single)).astype(jnp.bfloat16)
    state = widen(embedded) + tile_table[positions][:, None, :]
    normed = layer_norm(state, ln1_gain, ln1_bias)
    joint = jnp.einsum('btd,dc->btc', widen(normed), qkv_weight.reshape(D, -1).astype(single)).astype(jnp.bfloat16)
    joint = widen(joint).reshape(BAL, TILE_TOK, 3, HEADS, HEAD_DIM)
    scores = jnp.einsum('bqhd,bkhd->bhqk', joint[:, :, 0], joint[:, :, 1]) * HEAD_DIM ** (-0.5)
    weights = widen(jax.nn.softmax(scores, axis=-1).astype(jnp.bfloat16))
    context = jnp.einsum('bhqk,bkhd->bqhd', weights, joint[:, :, 2]).astype(jnp.bfloat16)
    context = widen(context).reshape(BAL, TILE_TOK, HEADS * HEAD_DIM)
    state = state + jnp.einsum('btc,cd->btd', context, out_weight.astype(single))
    normed = layer_norm(state, ln2_gain, ln2_bias)
    inner = jnp.einsum('btd,df->btf', widen(normed), fc1_weight.astype(single)) + fc1_bias
    hidden = jax.nn.gelu(inner, approximate=False).astype(jnp.bfloat16)
    state = state + jnp.einsum('btf,fd->btd', widen(hidden), fc2_weight.astype(single)) + fc2_bias
    normed = layer_norm(state, ln3_gain, ln3_bias)
    both = jnp.einsum('btd,dkc->btkc', widen(normed), kv_weight.astype(single))
    keys = both[:, :, 0].reshape(BAL, TILE_TOK, KV_HEADS, KV_DIM)
    keys = keys * lax.rsqrt(lax.optimization_barrier(jnp.mean(keys * keys, axis=-1, keepdims=True)) + 1e-05) * knorm_gain
    keys = keys.reshape(BAL, TILE_TOK, KV_HEADS * KV_DIM)
    return jnp.stack([keys, both[:, :, 1]], axis=2).astype(jnp.bfloat16)

def reference(tiles, tile_index, tile_from, patch_weight, tile_table, ln1_gain, ln1_bias, qkv_weight, out_weight, ln2_gain, ln2_bias, fc1_weight, fc1_bias, fc2_weight, fc2_bias, ln3_gain, ln3_bias, kv_weight, knorm_gain, page_owner, page_slot):
    work = tiles[tile_from].reshape(N_DP, BAL, TILE_TOK, PATCH)
    positions = tile_index[tile_from].reshape(N_DP, BAL)

    def one_rank(inputs):
        return encode_rank(inputs[0], inputs[1], patch_weight, tile_table, ln1_gain, ln1_bias, qkv_weight, out_weight, ln2_gain, ln2_bias, fc1_weight, fc1_bias, fc2_weight, fc2_bias, ln3_gain, ln3_bias, kv_weight, knorm_gain)
    encoded = lax.map(one_rank, (work, positions))
    pages = encoded.reshape(N_DP * P_DEV, PAGE, 2, KV_HEADS * KV_DIM)
    cache = jnp.zeros((N_DP * CSLOTS, PAGE, 2, KV_HEADS * KV_DIM), jnp.bfloat16)
    return cache.at[page_owner * CSLOTS + page_slot].set(pages)
```

```python
import functools

import jax
import jax.numpy as jnp
from jax import lax
from jax.experimental import pallas as pl
from jax.experimental.pallas import tpu as pltpu
from jax.sharding import PartitionSpec as P

HEAD_DIM = 80
KV_DIM = 128
PAGE = 16
CHUNKS = 4
F32 = jnp.float32
BF16 = jnp.bfloat16


def normalise(x, gain, bias):
    mean = jnp.mean(x, axis=-1, keepdims=True)
    centred = x - mean
    spread = jnp.mean(centred * centred, axis=-1, keepdims=True)
    return (centred * lax.rsqrt(spread + 1e-05) * gain + bias).astype(BF16)


def dot(a, b):
    return jnp.dot(a, b, preferred_element_type=F32)


def dot_t(a, b):
    return lax.dot_general(a, b, (((1,), (1,)), ((), ())), preferred_element_type=F32)


def wide(total):
    return 256 if total % 256 == 0 else total


def kernel(
    ranks,
    cap,
    from_ref,
    order_ref,
    ints_ref,
    tiles_ref,
    patch_ref,
    table_ref,
    g1_ref,
    b1_ref,
    g2_ref,
    b2_ref,
    g3_ref,
    b3_ref,
    fb1_ref,
    fb2_ref,
    kg_ref,
    wq_hbm,
    wk_hbm,
    wv_hbm,
    wo_hbm,
    w1_hbm,
    w2_hbm,
    wkv_hbm,
    out_ref,
    wq,
    wk,
    wv,
    wo,
    w1,
    w2,
    wkv,
    patch,
    ints_in,
    tile_out,
    tile_in,
    pix,
    state,
    n1,
    n2,
    n3,
    q_s,
    k_s,
    v_s,
    ctx,
    hid,
    acc,
    sib_out,
    sib_in,
    x_out,
    x_in,
    kvp,
    page_out,
    page_in,
    source_v,
    source_s,
    wsem,
    ints_sem,
    tile_sem,
    page_sem,
    patch_sem,
    pix_sem,
    sib_sem,
    x_sem,
    n_sem,
    s_sem,
):
    me = lax.axis_index("dp")
    t = lax.axis_index("tensor")
    core = lax.rem(t, 2)
    other = 1 - core
    sib = t + 1 - 2 * core
    far = lax.rem(t + 2, 4)
    far_sib = lax.rem(sib + 2, 4)
    hold, toks, width = tiles_ref.shape
    balanced = from_ref.shape[0] // ranks
    length = state.shape[0]
    dim = state.shape[1]
    rows = length // CHUNKS
    local_cols = wq.shape[1]
    heads = local_cols // HEAD_DIM

    weights = [
        (wq_hbm, wq),
        (wk_hbm, wk),
        (wv_hbm, wv),
        (wo_hbm, wo),
        (w1_hbm, w1),
        (w2_hbm, w2),
        (wkv_hbm, wkv),
    ]
    loads = [pltpu.make_async_copy(a, b, wsem.at[i]) for i, (a, b) in enumerate(weights)]
    for load in loads:
        load.start()

    barrier = pltpu.get_barrier_semaphore()
    for peer in (sib, far):
        pl.semaphore_signal(barrier, inc=1, device_id={"tensor": peer})
    for k in range(1, ranks):
        pl.semaphore_signal(barrier, inc=1, device_id={"dp": lax.rem(me + k, ranks)})
    pl.semaphore_wait(barrier, ranks + 1)

    def push(src, dst, sems, i, where):
        copy = pltpu.make_async_remote_copy(
            src_ref=src,
            dst_ref=dst,
            send_sem=sems.at[0, i],
            recv_sem=sems.at[1, i],
            device_id=where,
        )
        copy.start()
        return copy

    pending = []

    tile_copies, ints_copies = [None], [None]
    ints_in[0] = ints_ref[me]
    for k in range(1, ranks):
        dst = lax.rem(me + k, ranks)
        slot = jnp.int32(0)
        for s in range(balanced):
            v = from_ref[dst * balanced + s]
            slot = jnp.where(v // hold == me, v % hold, slot)
        tile_out[k] = tiles_ref[slot]
        ints_copies.append(push(ints_ref.at[dst], ints_in.at[k], ints_sem, k, {"dp": dst}))
        tile_copies.append(push(tile_out.at[k], tile_in.at[k], tile_sem, k, {"dp": dst}))

    cols = patch_ref.shape[0]
    patch[0] = patch_ref[...]
    p_sib = push(patch_ref, patch.at[1], patch_sem, 0, {"tensor": sib})
    p_far = push(patch_ref, patch.at[2], patch_sem, 1, {"tensor": far})
    for k in range(1, ranks):
        ints_copies[k].wait_recv()
        tile_copies[k].wait_recv()
    p_far.wait_recv()
    p_fwd = push(patch.at[2], patch.at[3], patch_sem, 2, {"tensor": sib})

    positions = []
    lane = lax.broadcasted_iota(jnp.int32, (8, 128), 1)
    row = lax.broadcasted_iota(jnp.int32, (8, 128), 0)
    for s in range(balanced):
        v = from_ref[me * balanced + s]
        src = v // hold
        slot = v % hold
        behind = lax.rem(me - src + ranks, ranks)
        mine = (src == me).astype(F32)
        own = tiles_ref[slot].astype(F32)
        came = tile_in[behind].astype(F32)
        pix[0, s] = jnp.where(mine > 0.5, own, came).astype(BF16)
        found = jnp.where((row == 1) & (lane == slot), ints_in[behind], 0).astype(F32)
        place = jnp.sum(jnp.sum(found, axis=1, keepdims=True), axis=0, keepdims=True)
        line = jnp.zeros((1, dim), F32)
        for m in range(table_ref.shape[0]):
            line = line + jnp.where(place == float(m), table_ref[m : m + 1, :], 0.0)
        positions.append(line)
    x_sib = push(pix.at[0], pix.at[1], pix_sem, 0, {"tensor": sib})
    x_far = push(pix.at[0], pix.at[2], pix_sem, 1, {"tensor": far})

    slots_here = out_ref.shape[0]
    want = lax.broadcasted_iota(jnp.int32, (slots_here, 128), 0)
    lanes = lax.broadcasted_iota(jnp.int32, (slots_here, 128), 1)
    index = jnp.zeros((slots_here, 128), jnp.int32)
    for k in range(ranks):
        hit = (want == ints_in[k, 0:1, :]) & (lanes < cap)
        index = index + jnp.where(hit, k * cap + lanes + 1, 0)
    index = jnp.sum(index, axis=1, keepdims=True) - 1
    source_v[...] = jnp.broadcast_to(index, (slots_here, 128))
    to_scalar = pltpu.make_async_copy(source_v, source_s, s_sem.at[0])
    to_scalar.start()

    x_far.wait_recv()
    x_fwd = push(pix.at[2], pix.at[3], pix_sem, 2, {"tensor": sib})
    p_sib.wait_recv()
    p_fwd.wait_recv()
    x_sib.wait_recv()
    x_fwd.wait_recv()
    pending += [p_sib, p_far, p_fwd, x_sib, x_far, x_fwd]
    pending += tile_copies[1:] + ints_copies[1:]

    which = (t, sib, far, far_sib)

    full = jnp.concatenate
    for s in range(balanced):
        base = positions[s]
        for i in range(4):
            parts = []
            for j in range(4):
                rel = jnp.int32(0)
                for m in range(1, 4):
                    rel = jnp.where(which[m] == j, m, rel)
                parts.append(dot_t(pix[i, s], patch[rel]).astype(BF16).astype(F32))
            x = full(parts, axis=1) + base
            at = pl.multiple_of(which[i] * toks, toks)
            n1[s, pl.ds(at, toks), :] = normalise(x, g1_ref[...], b1_ref[...])

            @pl.when(core == s)
            def _():
                state[pl.ds(at, toks), :] = x

    for i in range(3):
        loads[i].wait()
    for b in range(2):
        act = n1[b]
        q_s[b] = dot(act, wq[...]).astype(BF16)
        k_s[b] = dot(act, wk[...]).astype(BF16)
        v_s[b] = dot(act, wv[...]).astype(BF16)

    head_lane = lax.broadcasted_iota(jnp.int32, (1, local_cols), 1)
    masks = [
        ((head_lane >= h * HEAD_DIM) & (head_lane < (h + 1) * HEAD_DIM)).astype(F32)
        for h in range(heads)
    ]

    def attend(b):
        q = q_s[b]
        keys = k_s[b]
        vals = v_s[b]
        total = jnp.zeros((length, local_cols), F32)
        for h in range(heads):
            qh = q * masks[h].astype(BF16)
            scores = dot_t(qh, keys) * HEAD_DIM ** (-0.5)
            top = jnp.max(scores, axis=-1, keepdims=True)
            e = jnp.exp(scores - top)
            p = (e / jnp.sum(e, axis=-1, keepdims=True)).astype(BF16)
            total = total + dot(p, vals) * masks[h]
        ctx[b] = total.astype(BF16)

    step = wide(dim)

    def merge(layer, source, weight, gain, bias, extra, normed):
        left = source[other]

        @pl.loop(0, dim // step)
        def _(j):
            at = pl.ds(pl.multiple_of(j * step, step), step)
            sib_out[layer, :, at] = dot(left, weight[:, at]).astype(BF16)

        first = []
        for r in range(CHUNKS):
            at = pl.ds(r * rows, rows)
            first.append(
                push(
                    sib_out.at[layer, at],
                    sib_in.at[layer, at],
                    sib_sem,
                    layer * CHUNKS + r,
                    {"tensor": sib},
                )
            )
        return first

    def merge_rest(layer, first, source, weight, gain, bias, extra, normed):
        right = source[core]

        @pl.loop(0, dim // step)
        def _(j):
            at = pl.ds(pl.multiple_of(j * step, step), step)
            acc[:, at] = dot(right, weight[:, at])

        second, third = [], []
        for r in range(CHUNKS):
            at = pl.ds(r * rows, rows)
            first[r].wait_recv()
            both = acc[at, :] + sib_in[layer, at, :].astype(F32)
            acc[at, :] = both
            x_out[layer, at, :] = both.astype(BF16)
            second.append(
                push(
                    x_out.at[layer, at],
                    x_in.at[layer, at],
                    x_sem,
                    layer * CHUNKS + r,
                    {"tensor": far},
                )
            )
        for r in range(CHUNKS):
            at = pl.ds(r * rows, rows)
            second[r].wait_recv()
            x = state[at, :] + (acc[at, :] + x_in[layer, at, :].astype(F32)) + extra
            state[at, :] = x
            normed[core, at, :] = normalise(x, gain[...], bias[...])
            third.append(
                push(
                    normed.at[core, at],
                    normed.at[core, at],
                    n_sem,
                    layer * CHUNKS + r,
                    {"tensor": sib},
                )
            )
        pending.extend(first + second + third)
        return third

    attend(other)
    loads[3].wait()
    args = (ctx, wo, g2_ref, b2_ref, 0.0, n2)
    first = merge(0, *args)
    attend(core)
    third = merge_rest(0, first, *args)

    loads[4].wait()
    loads[5].wait()
    ff = w1.shape[1]
    ff_step = wide(ff)

    def up(b):
        act = n2[b]

        @pl.loop(0, ff // ff_step)
        def _(j):
            at = pl.ds(pl.multiple_of(j * ff_step, ff_step), ff_step)
            inner = dot(act, w1[:, at]) + fb1_ref[:, at]
            gelu = inner * (1.0 + lax.erf(inner * (0.5**0.5))) * 0.5
            hid[b, :, at] = gelu.astype(BF16)

    up(core)
    for copy in third:
        copy.wait_recv()
    up(other)
    args = (hid, w2, g3_ref, b3_ref, fb2_ref[...], n3)
    first = merge(1, *args)
    third = merge_rest(1, first, *args)

    loads[6].wait()
    half = wkv.shape[1] // 2

    def pages(b):
        both = dot(n3[b], wkv[...])
        parts = []
        for h in range(half // KV_DIM):
            key = both[:, h * KV_DIM : (h + 1) * KV_DIM]
            size = jnp.mean(key * key, axis=-1, keepdims=True)
            parts.append(key * lax.rsqrt(size + 1e-05) * kg_ref[...])
        parts.append(both[:, half:])
        joined = full(parts, axis=1)
        per = length // PAGE
        kvp[pl.ds(b * per, per)] = joined.reshape(per, PAGE, 2 * half).astype(BF16)

    pages(core)
    for copy in third:
        copy.wait_recv()
    pages(other)

    to_scalar.wait()
    page_copies = []
    for k in list(range(1, ranks)) + [0]:
        dst = lax.rem(me + k, ranks)
        for j in range(cap):
            page = kvp[order_ref[dst * cap + j]]
            if k:
                page_out[k, j] = page
            else:
                page_in[0, j] = page
        if k:
            page_copies.append(push(page_out.at[k], page_in.at[k], page_sem, k, {"dp": dst}))
    for copy in page_copies:
        copy.wait_recv()
    pending.extend(page_copies)

    @pl.loop(0, slots_here)
    def _(m):
        at = source_s[m, 0]
        safe = jnp.clip(at, 0, ranks * cap - 1)
        page = page_in[safe // cap, safe % cap].astype(F32)
        out_ref[m] = jnp.where(at >= 0, page, 0.0).astype(BF16)

    for copy in pending:
        copy.wait_send()


def on_device(
    tiles,
    tile_index,
    tile_from,
    patch_weight,
    tile_table,
    ln1_gain,
    ln1_bias,
    qkv_weight,
    out_weight,
    ln2_gain,
    ln2_bias,
    fc1_weight,
    fc1_bias,
    fc2_weight,
    fc2_bias,
    ln3_gain,
    ln3_bias,
    kv_weight,
    knorm_gain,
    page_owner,
    page_slot,
):
    ranks = lax.axis_size("dp")
    hold, toks, patch = tiles.shape
    balanced = tile_from.shape[0] // ranks
    shards = lax.axis_size("tensor")
    length = toks * shards
    dim = out_weight.shape[1]
    page_count = page_owner.shape[0]
    cap = max(2, 2 * ((page_count + ranks - 1) // ranks))
    cache_slots = 2 * page_count

    numbers = jnp.arange(page_count, dtype=jnp.int32)
    earlier = (page_owner[:, None] == page_owner[None, :]) & (numbers[None, :] < numbers[:, None])
    target = page_owner * cap + jnp.sum(earlier.astype(jnp.int32), axis=1)
    places = jnp.arange(ranks * cap, dtype=jnp.int32)
    routed = target[None, :] == places[:, None]
    order = jnp.sum(jnp.where(routed, numbers[None, :], 0), axis=1)
    going = jnp.sum(jnp.where(routed, page_slot[None, :] + 1, 0), axis=1) - 1
    ints = jnp.concatenate(
        [
            jnp.pad(going.reshape(ranks, 1, cap), ((0, 0), (0, 0), (0, 128 - cap)), constant_values=-1),
            jnp.broadcast_to(jnp.pad(tile_index, (0, 128 - hold))[None, None, :], (ranks, 1, 128)),
            jnp.zeros((ranks, 6, 128), jnp.int32),
        ],
        axis=1,
    )
    padded = -(-patch // 128) * 128
    tiles = jnp.pad(tiles, ((0, 0), (0, 0), (0, padded - patch)))
    patch_t = jnp.pad(patch_weight, ((0, padded - patch), (0, 0))).T
    local = qkv_weight.shape[2]
    ff = fc1_weight.shape[1]
    kv_cols = 2 * kv_weight.shape[2]
    wkv = kv_weight.reshape(dim, kv_cols)
    vmem = pl.BlockSpec(memory_space=pltpu.VMEM)
    smem = pl.BlockSpec(memory_space=pltpu.SMEM)
    anywhere = pl.BlockSpec(memory_space=pl.ANY)

    def sems(count):
        return pltpu.SemaphoreType.DMA((2, count))

    pairs = 2 * CHUNKS
    kept = (2, length, dim)
    cache = pl.pallas_call(
        functools.partial(kernel, ranks, cap),
        out_shape=jax.ShapeDtypeStruct((cache_slots, PAGE, kv_cols), BF16),
        in_specs=[smem] * 2 + [vmem] * 13 + [anywhere] * 7,
        out_specs=vmem,
        scratch_shapes=[
            pltpu.VMEM((dim, local), BF16),
            pltpu.VMEM((dim, local), BF16),
            pltpu.VMEM((dim, local), BF16),
            pltpu.VMEM((local, dim), BF16),
            pltpu.VMEM((dim, ff), BF16),
            pltpu.VMEM((ff, dim), BF16),
            pltpu.VMEM((dim, kv_cols), BF16),
            pltpu.VMEM((shards,) + patch_t.shape, BF16),
            pltpu.VMEM((ranks, 8, 128), jnp.int32),
            pltpu.VMEM((ranks, toks, padded), BF16),
            pltpu.VMEM((ranks, toks, padded), BF16),
            pltpu.VMEM((shards, balanced, toks, padded), BF16),
            pltpu.VMEM((length, dim), F32),
            pltpu.VMEM(kept, BF16),
            pltpu.VMEM(kept, BF16),
            pltpu.VMEM(kept, BF16),
            pltpu.VMEM((2, length, local), BF16),
            pltpu.VMEM((2, length, local), BF16),
            pltpu.VMEM((2, length, local), BF16),
            pltpu.VMEM((2, length, local), BF16),
            pltpu.VMEM((2, length, ff), BF16),
            pltpu.VMEM((length, dim), F32),
            pltpu.VMEM(kept, BF16),
            pltpu.VMEM(kept, BF16),
            pltpu.VMEM(kept, BF16),
            pltpu.VMEM(kept, BF16),
            pltpu.VMEM((page_count, PAGE, kv_cols), BF16),
            pltpu.VMEM((ranks, cap, PAGE, kv_cols), BF16),
            pltpu.VMEM((ranks, cap, PAGE, kv_cols), BF16),
            pltpu.VMEM((cache_slots, 128), jnp.int32),
            pltpu.SMEM((cache_slots, 128), jnp.int32),
            pltpu.SemaphoreType.DMA((7,)),
            sems(ranks),
            sems(ranks),
            sems(ranks),
            sems(3),
            sems(3),
            sems(pairs),
            sems(pairs),
            sems(pairs),
            pltpu.SemaphoreType.DMA((1,)),
        ],
        compiler_params=pltpu.CompilerParams(
            collective_id=0, has_side_effects=True, vmem_limit_bytes=56 * 1024 * 1024
        ),
        name="encoder",
    )(
        tile_from,
        order,
        ints,
        tiles,
        patch_t,
        tile_table,
        ln1_gain[None],
        ln1_bias[None],
        ln2_gain[None],
        ln2_bias[None],
        ln3_gain[None],
        ln3_bias[None],
        fc1_bias[None],
        fc2_bias[None],
        knorm_gain[None],
        qkv_weight[:, 0],
        qkv_weight[:, 1],
        qkv_weight[:, 2],
        out_weight,
        fc1_weight,
        fc2_weight,
        wkv,
    )
    return cache.reshape(cache_slots, PAGE, 2, kv_cols // 2)


def solution(mesh):
    return jax.shard_map(
        on_device,
        mesh=mesh,
        in_specs=(
            P(("groups", "dp"), "tensor", None),
            P(("groups", "dp")),
            P("groups"),
            P(None, "tensor"),
            P(),
            P(),
            P(),
            P(None, None, "tensor"),
            P("tensor", None),
            P(),
            P(),
            P(None, "tensor"),
            P("tensor"),
            P("tensor", None),
            P(),
            P(),
            P(),
            P(None, None, "tensor"),
            P(),
            P(("groups", "dp")),
            P(("groups", "dp")),
        ),
        out_specs=P(("groups", "dp"), None, None, "tensor"),
        check_vma=False,
    )
```

```python
import functools

import jax
import jax.numpy as jnp
from jax import lax
from jax.experimental import pallas as pl
from jax.experimental.pallas import tpu as pltpu
from jax.sharding import PartitionSpec as P

HEAD_DIM = 80
KV_DIM = 128
PAGE = 16
CHUNKS = 4
F32 = jnp.float32
BF16 = jnp.bfloat16


def normalise(x, gain, bias):
    mean = jnp.mean(x, axis=-1, keepdims=True)
    centred = x - mean
    spread = jnp.mean(centred * centred, axis=-1, keepdims=True)
    return (centred * lax.rsqrt(spread + 1e-05) * gain + bias).astype(BF16)


def dot(a, b):
    return jnp.dot(a, b, preferred_element_type=F32)


def dot_t(a, b):
    return lax.dot_general(a, b, (((1,), (1,)), ((), ())), preferred_element_type=F32)


def wide(total):
    return 256 if total % 256 == 0 else total


def kernel(
    ranks,
    cap,
    from_ref,
    position_ref,
    owner_ref,
    slot_ref,
    tiles_ref,
    patch_ref,
    table_ref,
    g1_in,
    b1_in,
    g2_in,
    b2_in,
    g3_in,
    b3_in,
    fb2_in,
    fb1_in,
    kg_ref,
    wqkv_hbm,
    wo_hbm,
    w1_hbm,
    w2_hbm,
    wkv_hbm,
    out_ref,
    wqkv,
    wo,
    w1,
    w2,
    wkv,
    patch,
    ints_out,
    ints_in,
    order_v,
    order_s,
    vec,
    fb1_ref,
    tile_out,
    tile_in,
    pix,
    state,
    n1,
    n2,
    n3,
    q_s,
    k_s,
    v_s,
    ctx,
    hid,
    acc,
    sib_out,
    sib_in,
    x_out,
    x_in,
    kvp,
    page_out,
    page_in,
    source_v,
    source_s,
    wsem,
    ints_sem,
    tile_sem,
    page_sem,
    patch_sem,
    pix_sem,
    sib_sem,
    x_sem,
    n_sem,
    s_sem,
):
    me = lax.axis_index("dp")
    t = lax.axis_index("tensor")
    core = lax.rem(t, 2)
    other = 1 - core
    sib = t + 1 - 2 * core
    far = lax.rem(t + 2, 4)
    far_sib = lax.rem(sib + 2, 4)
    hold, toks, width = tiles_ref.shape
    balanced = from_ref.shape[0] // ranks
    length = state.shape[0]
    dim = state.shape[1]
    rows = length // CHUNKS
    local_cols = wqkv.shape[1]
    heads = local_cols // HEAD_DIM

    weights = [
        (wqkv_hbm, wqkv),
        (wo_hbm, wo),
        (w1_hbm, w1),
        (w2_hbm, w2),
        (wkv_hbm, wkv),
    ]
    loads = [pltpu.make_async_copy(a, b, wsem.at[i]) for i, (a, b) in enumerate(weights)]
    for load in loads:
        load.start()

    barrier = pltpu.get_barrier_semaphore()
    for peer in (sib, far):
        pl.semaphore_signal(barrier, inc=1, device_id={"tensor": peer})
    for k in range(1, ranks):
        pl.semaphore_signal(barrier, inc=1, device_id={"dp": lax.rem(me + k, ranks)})
    pl.semaphore_wait(barrier, ranks + 1)

    def push(src, dst, sems, i, where):
        copy = pltpu.make_async_remote_copy(
            src_ref=src,
            dst_ref=dst,
            send_sem=sems.at[0, i],
            recv_sem=sems.at[1, i],
            device_id=where,
        )
        copy.start()
        return copy

    pending = []

    width_r = order_v.shape[0]
    row = lax.broadcasted_iota(jnp.int32, (width_r, 128), 0)
    lane = lax.broadcasted_iota(jnp.int32, (width_r, 128), 1)

    def assign(p, carry):
        count, order, going = carry
        owned = row == owner_ref[p]
        hit = owned & (lane == count)
        order = jnp.where(hit, p, order)
        going = jnp.where(hit, slot_ref[p], going)
        return count + jnp.where(owned, 1, 0), order, going

    zero = jnp.zeros((width_r, 128), jnp.int32)
    _, order, going = lax.fori_loop(0, owner_ref.shape[0], assign, (zero, zero, zero - 1))
    order_v[...] = order
    to_scalar = [pltpu.make_async_copy(order_v, order_s, s_sem.at[1])]
    to_scalar[0].start()
    ints_out[0:width_r, :] = going
    spots = jnp.zeros((8, 128), jnp.int32)
    lane8 = lax.broadcasted_iota(jnp.int32, (8, 128), 1)
    for i in range(hold):
        spots = jnp.where(lane8 == i, position_ref[i], spots)
    ints_out[width_r : width_r + 8, :] = spots
    ints_in[0] = ints_out[...]

    tile_copies, ints_copies = [None], [None]
    for k in range(1, ranks):
        dst = lax.rem(me + k, ranks)
        slot = jnp.int32(0)
        for s in range(balanced):
            v = from_ref[dst * balanced + s]
            slot = jnp.where(v // hold == me, v % hold, slot)
        tile_out[k] = tiles_ref[slot]
        ints_copies.append(push(ints_out, ints_in.at[k], ints_sem, k, {"dp": dst}))
        tile_copies.append(push(tile_out.at[k], tile_in.at[k], tile_sem, k, {"dp": dst}))

    patch[t] = patch_ref[...]
    p_sib = push(patch_ref, patch.at[t], patch_sem, 0, {"tensor": sib})
    p_far = push(patch_ref, patch.at[t], patch_sem, 1, {"tensor": far})
    for i, ref in enumerate((g1_in, b1_in, g2_in, b2_in, g3_in, b3_in, fb2_in)):
        vec[i : i + 1, :] = ref[...].reshape(1, dim)
    fb1_ref[...] = fb1_in[...].reshape(fb1_ref.shape)
    g1, b1, g2, b2, g3, b3, fb2 = [vec.at[i : i + 1] for i in range(7)]
    for k in range(1, ranks):
        ints_copies[k].wait_recv()
        tile_copies[k].wait_recv()

    positions = []
    row8 = lax.broadcasted_iota(jnp.int32, (8, 128), 0)
    for s in range(balanced):
        v = from_ref[me * balanced + s]
        src = v // hold
        slot = v % hold
        behind = lax.rem(me - src + ranks, ranks)
        mine = (src == me).astype(F32)
        own = tiles_ref[slot].astype(F32)
        came = tile_in[behind].astype(F32)
        pix[t, s * toks : (s + 1) * toks, :] = jnp.where(mine > 0.5, own, came).astype(BF16)
        found = jnp.where(
            (row8 == 0) & (lane8 == slot), ints_in[behind, width_r : width_r + 8, :], 0
        ).astype(F32)
        place = jnp.sum(jnp.sum(found, axis=1, keepdims=True), axis=0, keepdims=True)
        line = jnp.zeros((1, dim), F32)
        for m in range(table_ref.shape[0]):
            line = line + jnp.where(place == float(m), table_ref[m : m + 1, :], 0.0)
        positions.append(line)
    x_sib = push(pix.at[t], pix.at[t], pix_sem, 0, {"tensor": sib})
    x_far = push(pix.at[t], pix.at[t], pix_sem, 1, {"tensor": far})
    p_far.wait_recv()
    p_fwd = push(patch.at[far], patch.at[far], patch_sem, 2, {"tensor": sib})

    slots_here = out_ref.shape[0]
    want = lax.broadcasted_iota(jnp.int32, (slots_here, 128), 0)
    lanes = lax.broadcasted_iota(jnp.int32, (slots_here, 128), 1)
    index = jnp.zeros((slots_here, 128), jnp.int32)
    for k in range(ranks):
        hit = (want == ints_in[k, pl.ds(me, 1), :]) & (lanes < cap)
        index = index + jnp.where(hit, k * cap + lanes + 1, 0)
    index = jnp.sum(index, axis=1, keepdims=True) - 1
    source_v[...] = jnp.broadcast_to(index, (slots_here, 128))
    to_scalar.append(pltpu.make_async_copy(source_v, source_s, s_sem.at[0]))
    to_scalar[1].start()

    full = jnp.concatenate
    p_sib.wait_recv()
    p_fwd.wait_recv()

    def embed(i):
        x = dot_t(pix[i], patch[...].reshape(dim, width)).astype(BF16).astype(F32)
        at = pl.ds(pl.multiple_of(i * toks, toks), toks)
        for s in range(balanced):
            y = x[s * toks : (s + 1) * toks] + positions[s]
            n1[s, at, :] = normalise(y, g1[...], b1[...])

            @pl.when(core == s)
            def _():
                state[at, :] = y

    embed(t)
    x_far.wait_recv()
    x_fwd = push(pix.at[far], pix.at[far], pix_sem, 2, {"tensor": sib})
    x_sib.wait_recv()
    embed(sib)
    embed(far)
    x_fwd.wait_recv()
    embed(far_sib)
    pending += [p_sib, p_far, p_fwd, x_sib, x_far, x_fwd]
    pending += tile_copies[1:] + ints_copies[1:]

    loads[0].wait()
    for b in range(2):
        act = n1[b]
        q_s[b] = dot_t(act, wqkv[0]).astype(BF16)
        k_s[b] = dot_t(act, wqkv[1]).astype(BF16)
        v_s[b] = dot_t(act, wqkv[2]).astype(BF16)

    head_lane = lax.broadcasted_iota(jnp.int32, (1, local_cols), 1)
    masks = [
        ((head_lane >= h * HEAD_DIM) & (head_lane < (h + 1) * HEAD_DIM)).astype(F32)
        for h in range(heads)
    ]

    def attend(b):
        q = q_s[b]
        keys = k_s[b]
        vals = v_s[b]
        total = jnp.zeros((length, local_cols), F32)
        for h in range(heads):
            qh = q * masks[h].astype(BF16)
            scores = dot_t(qh, keys) * HEAD_DIM ** (-0.5)
            top = jnp.max(scores, axis=-1, keepdims=True)
            e = jnp.exp(scores - top)
            p = (e / jnp.sum(e, axis=-1, keepdims=True)).astype(BF16)
            total = total + dot(p, vals) * masks[h]
        ctx[b] = total.astype(BF16)

    step = wide(dim)

    def project(layer, source, weight, lo, hi):
        span = pl.ds(lo * rows, (hi - lo) * rows)
        left = source[other, span, :]

        @pl.loop(0, dim // step)
        def _(j):
            at = pl.ds(pl.multiple_of(j * step, step), step)
            sib_out[layer, span, at] = dot(left, weight[:, at]).astype(BF16)

        copies = []
        for r in range(lo, hi):
            at = pl.ds(r * rows, rows)
            i = layer * CHUNKS + r
            copies.append(
                push(
                    sib_out.at[layer, at],
                    sib_in.at[layer, at],
                    sib_sem,
                    i,
                    {"tensor": sib},
                )
            )
        return copies

    def own(source, weight, lo, hi):
        span = pl.ds(lo * rows, (hi - lo) * rows)
        right = source[core, span, :]

        @pl.loop(0, dim // step)
        def _(j):
            at = pl.ds(pl.multiple_of(j * step, step), step)
            acc[span, at] = dot(right, weight[:, at])

    def cross(layer, near, lo, hi):
        copies = []
        for r in range(lo, hi):
            at = pl.ds(r * rows, rows)
            i = layer * CHUNKS + r
            near[r - lo].wait_recv()
            both = acc[at, :] + sib_in[layer, at, :].astype(F32)
            acc[at, :] = both
            x_out[layer, at, :] = both.astype(BF16)
            copies.append(
                push(x_out.at[layer, at], x_in.at[layer, at], x_sem, i, {"tensor": far})
            )
        pending.extend(near + copies)
        return copies

    def settle(layer, across, lo, hi, gain, bias, extra, normed):
        copies = []
        for r in range(lo, hi):
            at = pl.ds(r * rows, rows)
            i = layer * CHUNKS + r
            across[r].wait_recv()
            x = state[at, :] + (acc[at, :] + x_in[layer, at, :].astype(F32)) + extra
            state[at, :] = x
            normed[core, at, :] = normalise(x, gain[...], bias[...])
            copies.append(
                push(normed.at[core, at], normed.at[core, at], n_sem, i, {"tensor": sib})
            )
        pending.extend(copies)
        return copies

    attend(other)
    loads[1].wait()
    near = project(0, ctx, wo, 0, CHUNKS)
    attend(core)
    own(ctx, wo, 0, CHUNKS)
    across0 = cross(0, near, 0, CHUNKS)

    loads[2].wait()
    loads[3].wait()
    ff = w1.shape[1]
    ff_step = wide(ff)
    group = CHUNKS // 2

    def up(b, lo, hi):
        span = pl.ds(lo * rows, (hi - lo) * rows)
        act = n2[b, span, :]

        @pl.loop(0, ff // ff_step)
        def _(j):
            at = pl.ds(pl.multiple_of(j * ff_step, ff_step), ff_step)
            inner = dot(act, w1[:, at]) + fb1_ref[:, at]
            gelu = inner * (1.0 + lax.erf(inner * (0.5**0.5))) * 0.5
            hid[b, span, at] = gelu.astype(BF16)

    across1 = []
    for lo in range(0, CHUNKS, group):
        hi = lo + group
        came = settle(0, across0, lo, hi, g2, b2, 0.0, n2)
        up(core, lo, hi)
        for copy in came:
            copy.wait_recv()
        up(other, lo, hi)
        near = project(1, hid, w2, lo, hi)
        own(hid, w2, lo, hi)
        across1 += cross(1, near, lo, hi)

    loads[4].wait()
    half = wkv.shape[1] // 2

    def pages(b, lo, hi):
        count = (hi - lo) * rows
        both = dot(n3[b, pl.ds(lo * rows, count), :], wkv[...])
        parts = []
        for h in range(half // KV_DIM):
            key = both[:, h * KV_DIM : (h + 1) * KV_DIM]
            size = jnp.mean(key * key, axis=-1, keepdims=True)
            parts.append(key * lax.rsqrt(size + 1e-05) * kg_ref[...])
        parts.append(both[:, half:])
        joined = full(parts, axis=1)
        first = b * (length // PAGE) + lo * rows // PAGE
        kvp[pl.ds(first, count // PAGE)] = joined.reshape(count // PAGE, PAGE, 2 * half).astype(BF16)

    for lo in range(0, CHUNKS, group):
        hi = lo + group
        came = settle(1, across1, lo, hi, g3, b3, fb2[...], n3)
        pages(core, lo, hi)
        for copy in came:
            copy.wait_recv()
        pages(other, lo, hi)

    for copy in to_scalar:
        copy.wait()
    page_copies = []
    for k in list(range(1, ranks)) + [0]:
        dst = lax.rem(me + k, ranks)
        for j in range(cap):
            page = kvp[order_s[dst, j]]
            if k:
                page_out[k, j] = page
            else:
                page_in[0, j] = page
        if k:
            page_copies.append(push(page_out.at[k], page_in.at[k], page_sem, k, {"dp": dst}))
    for copy in page_copies:
        copy.wait_recv()
    pending.extend(page_copies)

    @pl.loop(0, slots_here)
    def _(m):
        at = source_s[m, 0]
        safe = jnp.clip(at, 0, ranks * cap - 1)
        page = page_in[safe // cap, safe % cap].astype(F32)
        out_ref[m] = jnp.where(at >= 0, page, 0.0).astype(BF16)

    for copy in pending:
        copy.wait_send()


def on_device(
    tiles,
    tile_index,
    tile_from,
    patch_weight,
    tile_table,
    ln1_gain,
    ln1_bias,
    qkv_weight,
    out_weight,
    ln2_gain,
    ln2_bias,
    fc1_weight,
    fc1_bias,
    fc2_weight,
    fc2_bias,
    ln3_gain,
    ln3_bias,
    kv_weight,
    knorm_gain,
    page_owner,
    page_slot,
):
    ranks = lax.axis_size("dp")
    hold, toks, patch = tiles.shape
    balanced = tile_from.shape[0] // ranks
    shards = lax.axis_size("tensor")
    length = toks * shards
    dim = out_weight.shape[1]
    page_count = page_owner.shape[0]
    cap = max(2, 2 * ((page_count + ranks - 1) // ranks))
    cache_slots = 2 * page_count
    owner_rows = -(-ranks // 8) * 8
    local = qkv_weight.shape[2]
    ff = fc1_weight.shape[1]
    kv_cols = 2 * kv_weight.shape[2]
    wkv = kv_weight.reshape(dim, kv_cols)
    vmem = pl.BlockSpec(memory_space=pltpu.VMEM)
    smem = pl.BlockSpec(memory_space=pltpu.SMEM)
    anywhere = pl.BlockSpec(memory_space=pl.ANY)

    def sems(count):
        return pltpu.SemaphoreType.DMA((2, count))

    pairs = 2 * CHUNKS
    kept = (2, length, dim)
    cache = pl.pallas_call(
        functools.partial(kernel, ranks, cap),
        out_shape=jax.ShapeDtypeStruct((cache_slots, PAGE, kv_cols), BF16),
        in_specs=[smem] * 4 + [vmem] * 12 + [anywhere] * 5,
        out_specs=vmem,
        scratch_shapes=[
            pltpu.VMEM((3, local, dim), BF16),
            pltpu.VMEM((local, dim), BF16),
            pltpu.VMEM((dim, ff), BF16),
            pltpu.VMEM((ff, dim), BF16),
            pltpu.VMEM((dim, kv_cols), BF16),
            pltpu.VMEM((shards, dim // shards, patch), BF16),
            pltpu.VMEM((owner_rows + 8, 128), jnp.int32),
            pltpu.VMEM((ranks, owner_rows + 8, 128), jnp.int32),
            pltpu.VMEM((owner_rows, 128), jnp.int32),
            pltpu.SMEM((owner_rows, 128), jnp.int32),
            pltpu.VMEM((8, dim), F32),
            pltpu.VMEM((1, ff), F32),
            pltpu.VMEM((ranks, toks, patch), BF16),
            pltpu.VMEM((ranks, toks, patch), BF16),
            pltpu.VMEM((shards, balanced * toks, patch), BF16),
            pltpu.VMEM((length, dim), F32),
            pltpu.VMEM(kept, BF16),
            pltpu.VMEM(kept, BF16),
            pltpu.VMEM(kept, BF16),
            pltpu.VMEM((2, length, local), BF16),
            pltpu.VMEM((2, length, local), BF16),
            pltpu.VMEM((2, length, local), BF16),
            pltpu.VMEM((2, length, local), BF16),
            pltpu.VMEM((2, length, ff), BF16),
            pltpu.VMEM((length, dim), F32),
            pltpu.VMEM(kept, BF16),
            pltpu.VMEM(kept, BF16),
            pltpu.VMEM(kept, BF16),
            pltpu.VMEM(kept, BF16),
            pltpu.VMEM((page_count, PAGE, kv_cols), BF16),
            pltpu.VMEM((ranks, cap, PAGE, kv_cols), BF16),
            pltpu.VMEM((ranks, cap, PAGE, kv_cols), BF16),
            pltpu.VMEM((cache_slots, 128), jnp.int32),
            pltpu.SMEM((cache_slots, 128), jnp.int32),
            pltpu.SemaphoreType.DMA((5,)),
            sems(ranks),
            sems(ranks),
            sems(ranks),
            sems(3),
            sems(3),
            sems(pairs),
            sems(pairs),
            sems(pairs),
            pltpu.SemaphoreType.DMA((2,)),
        ],
        compiler_params=pltpu.CompilerParams(
            collective_id=0, has_side_effects=True, vmem_limit_bytes=56 * 1024 * 1024
        ),
        name="encoder",
    )(
        tile_from,
        tile_index,
        page_owner,
        page_slot,
        tiles,
        patch_weight.T,
        tile_table,
        ln1_gain,
        ln1_bias,
        ln2_gain,
        ln2_bias,
        ln3_gain,
        ln3_bias,
        fc2_bias,
        fc1_bias,
        knorm_gain[None],
        qkv_weight.transpose(1, 2, 0),
        out_weight,
        fc1_weight,
        fc2_weight,
        wkv,
    )
    return cache.reshape(cache_slots, PAGE, 2, kv_cols // 2)


def solution(mesh):
    return jax.shard_map(
        on_device,
        mesh=mesh,
        in_specs=(
            P(("groups", "dp"), "tensor", None),
            P(("groups", "dp")),
            P("groups"),
            P(None, "tensor"),
            P(),
            P(),
            P(),
            P(None, None, "tensor"),
            P("tensor", None),
            P(),
            P(),
            P(None, "tensor"),
            P("tensor"),
            P("tensor", None),
            P(),
            P(),
            P(),
            P(None, None, "tensor"),
            P(),
            P(("groups", "dp")),
            P(("groups", "dp")),
        ),
        out_specs=P(("groups", "dp"), None, None, "tensor"),
        check_vma=False,
    )
```

```python
import functools

import jax
import jax.numpy as jnp
from jax import lax
from jax.experimental import pallas as pl
from jax.experimental.pallas import tpu as pltpu
from jax.sharding import PartitionSpec as P

HEAD_DIM = 80
KV_DIM = 128
PAGE = 16
CHUNKS = 4
F32 = jnp.float32
BF16 = jnp.bfloat16


def normalise(x, gain, bias):
    mean = jnp.mean(x, axis=-1, keepdims=True)
    centred = x - mean
    spread = jnp.mean(centred * centred, axis=-1, keepdims=True)
    return (centred * lax.rsqrt(spread + 1e-05) * gain + bias).astype(BF16)


def dot(a, b):
    return jnp.dot(a, b, preferred_element_type=F32)


def dot_t(a, b):
    return lax.dot_general(a, b, (((1,), (1,)), ((), ())), preferred_element_type=F32)


def wide(total):
    return 256 if total % 256 == 0 else total


def kernel(
    ranks,
    cap,
    from_ref,
    position_ref,
    owner_ref,
    slot_ref,
    tiles_ref,
    patch_ref,
    table_ref,
    g1_in,
    b1_in,
    g2_in,
    b2_in,
    g3_in,
    b3_in,
    fb2_in,
    fb1_in,
    kg_ref,
    wqkv_hbm,
    wo_hbm,
    w1_hbm,
    w2_hbm,
    wkv_hbm,
    out_ref,
    wqkv,
    wo,
    w1,
    w2,
    wkv_raw,
    wkv,
    patch,
    ints_out,
    ints_in,
    spots_out,
    spots_in,
    order_v,
    order_s,
    vec,
    fb1_ref,
    tile_out,
    tile_in,
    pix,
    state,
    n1,
    n2,
    n3,
    q_s,
    k_s,
    v_s,
    ctx,
    hid,
    acc,
    sib_out,
    sib_in,
    x_out,
    x_in,
    kvp,
    page_out,
    page_in,
    source_v,
    source_s,
    wsem,
    ints_sem,
    spot_sem,
    tile_sem,
    page_sem,
    patch_sem,
    pix_sem,
    sib_sem,
    x_sem,
    n_sem,
    s_sem,
):
    me = lax.axis_index("dp")
    t = lax.axis_index("tensor")
    core = lax.rem(t, 2)
    other = 1 - core
    sib = t + 1 - 2 * core
    far = lax.rem(t + 2, 4)
    far_sib = lax.rem(sib + 2, 4)
    hold, toks, width = tiles_ref.shape
    balanced = from_ref.shape[0] // ranks
    length = state.shape[0]
    dim = state.shape[1]
    rows = length // CHUNKS
    local_cols = wqkv.shape[1]
    heads = local_cols // HEAD_DIM

    weights = [
        (wqkv_hbm, wqkv),
        (wo_hbm, wo),
        (w1_hbm, w1),
        (w2_hbm, w2),
        (wkv_hbm, wkv_raw),
    ]
    loads = [pltpu.make_async_copy(a, b, wsem.at[i]) for i, (a, b) in enumerate(weights)]
    for load in loads:
        load.start()

    barrier = pltpu.get_barrier_semaphore()
    for peer in (sib, far):
        pl.semaphore_signal(barrier, inc=1, device_id={"tensor": peer})
    for k in range(1, ranks):
        pl.semaphore_signal(barrier, inc=1, device_id={"dp": lax.rem(me + k, ranks)})
    pl.semaphore_wait(barrier, ranks + 1)

    def push(src, dst, sems, i, where):
        copy = pltpu.make_async_remote_copy(
            src_ref=src,
            dst_ref=dst,
            send_sem=sems.at[0, i],
            recv_sem=sems.at[1, i],
            device_id=where,
        )
        copy.start()
        return copy

    pending = []

    lane8 = lax.broadcasted_iota(jnp.int32, (8, 128), 1)
    spots = jnp.zeros((8, 128), jnp.int32)
    for i in range(hold):
        spots = jnp.where(lane8 == i, position_ref[i], spots)
    spots_out[...] = spots
    spots_in[0] = spots
    tile_copies, spot_copies = [None], [None]
    for k in range(1, ranks):
        dst = lax.rem(me + k, ranks)
        slot = jnp.int32(0)
        for s in range(balanced):
            v = from_ref[dst * balanced + s]
            slot = jnp.where(v // hold == me, v % hold, slot)
        tile_out[k] = tiles_ref[slot]
        spot_copies.append(push(spots_out, spots_in.at[k], spot_sem, k, {"dp": dst}))
        tile_copies.append(push(tile_out.at[k], tile_in.at[k], tile_sem, k, {"dp": dst}))

    patch[t] = patch_ref[...]
    p_sib = push(patch_ref, patch.at[t], patch_sem, 0, {"tensor": sib})
    p_far = push(patch_ref, patch.at[t], patch_sem, 1, {"tensor": far})
    for i, ref in enumerate((g1_in, b1_in, g2_in, b2_in, g3_in, b3_in, fb2_in)):
        vec[i : i + 1, :] = ref[...].reshape(1, dim)
    fb1_ref[...] = fb1_in[...].reshape(fb1_ref.shape)
    g1, b1, g2, b2, g3, b3, fb2 = [vec.at[i : i + 1] for i in range(7)]
    for k in range(1, ranks):
        spot_copies[k].wait_recv()
        tile_copies[k].wait_recv()

    positions = []
    row8 = lax.broadcasted_iota(jnp.int32, (8, 128), 0)
    for s in range(balanced):
        v = from_ref[me * balanced + s]
        src = v // hold
        slot = v % hold
        behind = lax.rem(me - src + ranks, ranks)
        mine = (src == me).astype(F32)
        own = tiles_ref[slot].astype(F32)
        came = tile_in[behind].astype(F32)
        pix[t, s * toks : (s + 1) * toks, :] = jnp.where(mine > 0.5, own, came).astype(BF16)
        found = jnp.where(
            (row8 == 0) & (lane8 == slot), spots_in[behind], 0
        ).astype(F32)
        place = jnp.sum(jnp.sum(found, axis=1, keepdims=True), axis=0, keepdims=True)
        line = jnp.zeros((1, dim), F32)
        for m in range(table_ref.shape[0]):
            line = line + jnp.where(place == float(m), table_ref[m : m + 1, :], 0.0)
        positions.append(line)
    x_sib = push(pix.at[t], pix.at[t], pix_sem, 0, {"tensor": sib})
    x_far = push(pix.at[t], pix.at[t], pix_sem, 1, {"tensor": far})
    p_far.wait_recv()
    p_fwd = push(patch.at[far], patch.at[far], patch_sem, 2, {"tensor": sib})

    width_r = order_v.shape[0]
    row = lax.broadcasted_iota(jnp.int32, (width_r, 128), 0)
    lane = lax.broadcasted_iota(jnp.int32, (width_r, 128), 1)

    def assign(p, carry):
        count, order, going = carry
        owned = row == owner_ref[p]
        hit = owned & (lane == count)
        order = jnp.where(hit, p, order)
        going = jnp.where(hit, slot_ref[p], going)
        return count + jnp.where(owned, 1, 0), order, going

    zero = jnp.zeros((width_r, 128), jnp.int32)
    _, order, going = lax.fori_loop(0, owner_ref.shape[0], assign, (zero, zero, zero - 1))
    order_v[...] = order
    to_scalar = [pltpu.make_async_copy(order_v, order_s, s_sem.at[1])]
    to_scalar[0].start()
    ints_out[...] = going
    ints_in[0] = going
    ints_copies = [None]
    for k in range(1, ranks):
        dst = lax.rem(me + k, ranks)
        ints_copies.append(push(ints_out, ints_in.at[k], ints_sem, k, {"dp": dst}))

    full = jnp.concatenate
    p_sib.wait_recv()
    p_fwd.wait_recv()

    def embed(first, second):
        both = full([pix[first], pix[second]], axis=0)
        x = dot_t(both, patch[...].reshape(dim, width)).astype(BF16).astype(F32)
        for n, i in enumerate((first, second)):
            at = pl.ds(pl.multiple_of(i * toks, toks), toks)
            for s in range(balanced):
                low = (n * balanced + s) * toks
                y = x[low : low + toks] + positions[s]
                n1[s, at, :] = normalise(y, g1[...], b1[...])

                @pl.when(core == s)
                def _():
                    state[at, :] = y

    x_sib.wait_recv()
    embed(t, sib)
    x_far.wait_recv()
    x_fwd = push(pix.at[far], pix.at[far], pix_sem, 2, {"tensor": sib})
    x_fwd.wait_recv()
    embed(far, far_sib)
    pending += [p_sib, p_far, p_fwd, x_sib, x_far, x_fwd]
    pending += tile_copies[1:] + spot_copies[1:] + ints_copies[1:]

    loads[0].wait()
    act = n1[...].reshape(2 * length, dim)
    for i, kept in enumerate((q_s, k_s, v_s)):
        kept[...] = dot_t(act, wqkv[i]).astype(BF16).reshape(2, length, local_cols)

    head_lane = lax.broadcasted_iota(jnp.int32, (1, local_cols), 1)
    masks = [
        ((head_lane >= h * HEAD_DIM) & (head_lane < (h + 1) * HEAD_DIM)).astype(F32)
        for h in range(heads)
    ]

    def attend(b, lo, hi):
        span = pl.ds(lo * rows, (hi - lo) * rows)
        q = q_s[b, span, :]
        keys = k_s[b]
        vals = v_s[b]
        total = jnp.zeros(q.shape, F32)
        for h in range(heads):
            qh = q * masks[h].astype(BF16)
            scores = dot_t(qh, keys) * HEAD_DIM ** (-0.5)
            top = jnp.max(scores, axis=-1, keepdims=True)
            e = jnp.exp(scores - top)
            p = (e * (1.0 / jnp.sum(e, axis=-1, keepdims=True))).astype(BF16)
            total = total + dot(p, vals) * masks[h]
        ctx[b, span, :] = total.astype(BF16)

    step = wide(dim)

    def project(layer, source, weight, lo, hi):
        count = (hi - lo) * rows
        span = pl.ds(lo * rows, count)
        both = full([source[other, span, :], source[core, span, :]], axis=0)

        @pl.loop(0, dim // step)
        def _(j):
            at = pl.ds(pl.multiple_of(j * step, step), step)
            part = dot(both, weight[:, at])
            sib_out[layer, span, at] = part[:count].astype(BF16)
            acc[span, at] = part[count:]

        copies = []
        for r in range(lo, hi):
            at = pl.ds(r * rows, rows)
            i = layer * CHUNKS + r
            copies.append(
                push(
                    sib_out.at[layer, at],
                    sib_in.at[layer, at],
                    sib_sem,
                    i,
                    {"tensor": sib},
                )
            )
        return copies

    def cross(layer, near, lo, hi):
        copies = []
        for r in range(lo, hi):
            at = pl.ds(r * rows, rows)
            i = layer * CHUNKS + r
            near[r - lo].wait_recv()
            both = acc[at, :] + sib_in[layer, at, :].astype(F32)
            acc[at, :] = both
            x_out[layer, at, :] = both.astype(BF16)
            copies.append(
                push(x_out.at[layer, at], x_in.at[layer, at], x_sem, i, {"tensor": far})
            )
        pending.extend(near + copies)
        return copies

    def settle(layer, across, lo, hi, gain, bias, extra, normed):
        copies = []
        for r in range(lo, hi):
            at = pl.ds(r * rows, rows)
            i = layer * CHUNKS + r
            across[r].wait_recv()
            x = state[at, :] + (acc[at, :] + x_in[layer, at, :].astype(F32)) + extra
            state[at, :] = x
            normed[core, at, :] = normalise(x, gain[...], bias[...])
            copies.append(
                push(normed.at[core, at], normed.at[core, at], n_sem, i, {"tensor": sib})
            )
        pending.extend(copies)
        return copies

    group = CHUNKS // 2
    loads[1].wait()
    across0 = []
    for b in range(2):
        attend(b, 0, CHUNKS)
    for lo in range(0, CHUNKS, group):
        near = project(0, ctx, wo, lo, lo + group)
        across0 += cross(0, near, lo, lo + group)

    for copy in ints_copies[1:]:
        copy.wait_recv()
    slots_here = out_ref.shape[0]
    want = lax.broadcasted_iota(jnp.int32, (slots_here, 128), 0)
    lanes = lax.broadcasted_iota(jnp.int32, (slots_here, 128), 1)
    index = jnp.zeros((slots_here, 128), jnp.int32)
    for k in range(ranks):
        hit = (want == ints_in[k, pl.ds(me, 1), :]) & (lanes < cap)
        index = index + jnp.where(hit, k * cap + lanes + 1, 0)
    index = jnp.sum(index, axis=1, keepdims=True) - 1
    source_v[...] = jnp.broadcast_to(index, (slots_here, 128))
    to_scalar.append(pltpu.make_async_copy(source_v, source_s, s_sem.at[0]))
    to_scalar[1].start()

    loads[4].wait()
    kv_half = wkv_raw.shape[2]

    @pl.loop(0, wkv_raw.shape[0] // 64)
    def _(i):
        at = pl.ds(pl.multiple_of(i * 64, 64), 64)
        block = wkv_raw[at].astype(F32)
        wkv[at, 0:kv_half] = block[:, 0, :].astype(BF16)
        wkv[at, kv_half:] = block[:, 1, :].astype(BF16)

    loads[2].wait()
    loads[3].wait()
    ff = w1.shape[1]
    ff_step = wide(ff)

    def up(lo, hi):
        count = (hi - lo) * rows
        span = pl.ds(lo * rows, count)
        act = n2[:, span, :].reshape(2 * count, dim)

        @pl.loop(0, ff // ff_step)
        def _(j):
            at = pl.ds(pl.multiple_of(j * ff_step, ff_step), ff_step)
            inner = dot(act, w1[:, at]) + fb1_ref[:, at]
            gelu = inner * (1.0 + lax.erf(inner * (0.5**0.5))) * 0.5
            hid[:, span, at] = gelu.astype(BF16).reshape(2, count, ff_step)

    across1 = []
    for lo in range(0, CHUNKS, group):
        hi = lo + group
        came = settle(0, across0, lo, hi, g2, b2, 0.0, n2)
        for copy in came:
            copy.wait_recv()
        up(lo, hi)
        near = project(1, hid, w2, lo, hi)
        across1 += cross(1, near, lo, hi)

    half = wkv.shape[1] // 2

    def pages(lo, hi):
        count = (hi - lo) * rows
        both = dot(n3[:, pl.ds(lo * rows, count), :].reshape(2 * count, dim), wkv[...])
        parts = []
        for h in range(half // KV_DIM):
            key = both[:, h * KV_DIM : (h + 1) * KV_DIM]
            size = jnp.mean(key * key, axis=-1, keepdims=True)
            parts.append(key * lax.rsqrt(size + 1e-05) * kg_ref[...])
        parts.append(both[:, half:])
        joined = full(parts, axis=1).reshape(2, count // PAGE, PAGE, 2 * half).astype(BF16)
        for b in range(2):
            first = b * (length // PAGE) + lo * rows // PAGE
            kvp[pl.ds(first, count // PAGE)] = joined[b]

    for lo in range(0, CHUNKS, group):
        hi = lo + group
        came = settle(1, across1, lo, hi, g3, b3, fb2[...], n3)
        for copy in came:
            copy.wait_recv()
        pages(lo, hi)

    for copy in to_scalar:
        copy.wait()
    page_copies = []
    for k in list(range(1, ranks)) + [0]:
        dst = lax.rem(me + k, ranks)
        for j in range(cap):
            page = kvp[order_s[dst, j]]
            if k:
                page_out[k, j] = page
            else:
                page_in[0, j] = page
        if k:
            page_copies.append(push(page_out.at[k], page_in.at[k], page_sem, k, {"dp": dst}))
    for copy in page_copies:
        copy.wait_recv()
    pending.extend(page_copies)

    @pl.loop(0, slots_here)
    def _(m):
        at = source_s[m, 0]
        safe = jnp.clip(at, 0, ranks * cap - 1)
        page = page_in[safe // cap, safe % cap].astype(F32)
        out_ref[m] = jnp.where(at >= 0, page, 0.0).astype(BF16)

    for copy in pending:
        copy.wait_send()


def on_device(
    tiles,
    tile_index,
    tile_from,
    patch_weight,
    tile_table,
    ln1_gain,
    ln1_bias,
    qkv_weight,
    out_weight,
    ln2_gain,
    ln2_bias,
    fc1_weight,
    fc1_bias,
    fc2_weight,
    fc2_bias,
    ln3_gain,
    ln3_bias,
    kv_weight,
    knorm_gain,
    page_owner,
    page_slot,
):
    ranks = lax.axis_size("dp")
    hold, toks, patch = tiles.shape
    balanced = tile_from.shape[0] // ranks
    shards = lax.axis_size("tensor")
    length = toks * shards
    dim = out_weight.shape[1]
    page_count = page_owner.shape[0]
    cap = max(2, 2 * ((page_count + ranks - 1) // ranks))
    cache_slots = 2 * page_count
    owner_rows = -(-ranks // 8) * 8
    local = qkv_weight.shape[2]
    ff = fc1_weight.shape[1]
    kv_cols = 2 * kv_weight.shape[2]
    vmem = pl.BlockSpec(memory_space=pltpu.VMEM)
    smem = pl.BlockSpec(memory_space=pltpu.SMEM)
    anywhere = pl.BlockSpec(memory_space=pl.ANY)

    def sems(count):
        return pltpu.SemaphoreType.DMA((2, count))

    pairs = 2 * CHUNKS
    kept = (2, length, dim)
    cache = pl.pallas_call(
        functools.partial(kernel, ranks, cap),
        out_shape=jax.ShapeDtypeStruct((cache_slots, PAGE, kv_cols), BF16),
        in_specs=[smem] * 4 + [vmem] * 12 + [anywhere] * 5,
        out_specs=vmem,
        scratch_shapes=[
            pltpu.VMEM((3, local, dim), BF16),
            pltpu.VMEM((local, dim), BF16),
            pltpu.VMEM((dim, ff), BF16),
            pltpu.VMEM((ff, dim), BF16),
            pltpu.VMEM(kv_weight.shape, BF16),
            pltpu.VMEM((dim, kv_cols), BF16),
            pltpu.VMEM((shards, dim // shards, patch), BF16),
            pltpu.VMEM((owner_rows, 128), jnp.int32),
            pltpu.VMEM((ranks, owner_rows, 128), jnp.int32),
            pltpu.VMEM((8, 128), jnp.int32),
            pltpu.VMEM((ranks, 8, 128), jnp.int32),
            pltpu.VMEM((owner_rows, 128), jnp.int32),
            pltpu.SMEM((owner_rows, 128), jnp.int32),
            pltpu.VMEM((8, dim), F32),
            pltpu.VMEM((1, ff), F32),
            pltpu.VMEM((ranks, toks, patch), BF16),
            pltpu.VMEM((ranks, toks, patch), BF16),
            pltpu.VMEM((shards, balanced * toks, patch), BF16),
            pltpu.VMEM((length, dim), F32),
            pltpu.VMEM(kept, BF16),
            pltpu.VMEM(kept, BF16),
            pltpu.VMEM(kept, BF16),
            pltpu.VMEM((2, length, local), BF16),
            pltpu.VMEM((2, length, local), BF16),
            pltpu.VMEM((2, length, local), BF16),
            pltpu.VMEM((2, length, local), BF16),
            pltpu.VMEM((2, length, ff), BF16),
            pltpu.VMEM((length, dim), F32),
            pltpu.VMEM(kept, BF16),
            pltpu.VMEM(kept, BF16),
            pltpu.VMEM(kept, BF16),
            pltpu.VMEM(kept, BF16),
            pltpu.VMEM((page_count, PAGE, kv_cols), BF16),
            pltpu.VMEM((ranks, cap, PAGE, kv_cols), BF16),
            pltpu.VMEM((ranks, cap, PAGE, kv_cols), BF16),
            pltpu.VMEM((cache_slots, 128), jnp.int32),
            pltpu.SMEM((cache_slots, 128), jnp.int32),
            pltpu.SemaphoreType.DMA((5,)),
            sems(ranks),
            sems(ranks),
            sems(ranks),
            sems(ranks),
            sems(3),
            sems(3),
            sems(pairs),
            sems(pairs),
            sems(pairs),
            pltpu.SemaphoreType.DMA((2,)),
        ],
        compiler_params=pltpu.CompilerParams(
            collective_id=0, has_side_effects=True, vmem_limit_bytes=56 * 1024 * 1024
        ),
        name="encoder",
    )(
        tile_from,
        tile_index,
        page_owner,
        page_slot,
        tiles,
        patch_weight.T,
        tile_table,
        ln1_gain,
        ln1_bias,
        ln2_gain,
        ln2_bias,
        ln3_gain,
        ln3_bias,
        fc2_bias,
        fc1_bias,
        knorm_gain[None],
        qkv_weight.transpose(1, 2, 0),
        out_weight,
        fc1_weight,
        fc2_weight,
        kv_weight,
    )
    return cache.reshape(cache_slots, PAGE, 2, kv_cols // 2)


def solution(mesh):
    return jax.shard_map(
        on_device,
        mesh=mesh,
        in_specs=(
            P(("groups", "dp"), "tensor", None),
            P(("groups", "dp")),
            P("groups"),
            P(None, "tensor"),
            P(),
            P(),
            P(),
            P(None, None, "tensor"),
            P("tensor", None),
            P(),
            P(),
            P(None, "tensor"),
            P("tensor"),
            P("tensor", None),
            P(),
            P(),
            P(),
            P(None, None, "tensor"),
            P(),
            P(("groups", "dp")),
            P(("groups", "dp")),
        ),
        out_specs=P(("groups", "dp"), None, None, "tensor"),
        check_vma=False,
    )
```
